32 devices in a mesh: sub: 16 (over z, x, core), coarse: 2 (over y).
Axes of the slice: x: 2, y: 2, z: 4, core: 2. Of those that a mesh axis runs over, the one named last changes fastest.
Arguments:
- residual_parts: bfloat16 [16, 2, 4, 256, 512], P('sub', 'coarse'), may hold values from -6 to 6
- face_slot: int32 [16, 2, 4], P('sub', 'coarse'), may hold values from 0 to 3, each once within a row
- face_order: int32 [16, 2, 4, 512], P('sub', 'coarse'), may hold values from 0 to 511, each once within a row
- face_scale: float32 [16, 2, 4], P('sub', 'coarse'), may hold values from 0 to 1, as said below
- vertex_unknowns: int32 [16, 2, 256], P('sub', 'coarse'), may hold values from 0 to 2047, all different within a row
- front_inverse: bfloat16 [16, 2, 2048, 2048], P('sub', 'coarse')
- coarse_basis: bfloat16 [16, 2, 2048, 256], P('sub', 'coarse'), may hold values from -0.125 to 0.125
- coarse_inverse: bfloat16 [16, 512, 512], P('sub', None, 'coarse'), as said below
- thermal_handoff: bfloat16 [16, 512, 128], P('sub'), may hold values from -0.25 to 0.25
- chain_transfer: float32 [16, 128, 128], P('sub')
- coupling_in: bfloat16 [16, 128, 512], P('sub', None, 'coarse'), may hold values from -0.5 to 0.5
Outputs:
- correction: bfloat16 [16, 2, 4, 256, 512], P('sub', 'coarse')
The draws below stay inside these ranges and needn't reach their ends.
Inputs may be any that keep to these rules, and one draw needn't show every extreme that they name: `face_slot`: each row is a permutation of 0 to 3. `face_order`: each row is a permutation of 0 to 511. `vertex_unknowns`: the 256 entries of each subdomain are distinct. `face_scale`: the two weights of a shared face sum to one; a face on the outer boundary has weight one. `coarse_inverse`: each line's matrix is symmetric.
All inputs are finite; a program needn't handle non-finite values.
Results may differ from the reference program's by a relative error of at most 0.0059.
Values may be sent and summed in bfloat16 or wider, within the bound.
A program may use at most 128 MiB of HBM per device.

```python
import math
import jax
import jax.numpy as jnp
from jax import lax

FACE_DOFS = 512
VERTEX_COUNT = 256
CHANNELS = 128
SAMPLES = 256
N_SUB = 16
N_COARSE = 2


def draw_face_scale(key, part):
    top_level = math.log(100.0)
    stiffness = jnp.exp(jax.random.uniform(jax.random.fold_in(key, 11), (N_SUB, N_COARSE), jnp.float32, 0.0, top_level))
    lower = jnp.concatenate([stiffness[:1], stiffness[:-1]], 0)
    upper = jnp.concatenate([stiffness[1:], stiffness[-1:]], 0)
    left_side = jnp.concatenate([stiffness[:, :1], stiffness[:, :-1]], 1)
    right_side = jnp.concatenate([stiffness[:, 1:], stiffness[:, -1:]], 1)
    row_index = lax.broadcasted_iota(jnp.int32, (N_SUB, N_COARSE), 0)
    col_index = lax.broadcasted_iota(jnp.int32, (N_SUB, N_COARSE), 1)
    weights = [jnp.where(row_index > 0, stiffness / (stiffness + lower), 1.0), jnp.where(row_index < N_SUB - 1, stiffness / (stiffness + upper), 1.0), jnp.where(col_index > 0, stiffness / (stiffness + left_side), 1.0), jnp.where(col_index < N_COARSE - 1, stiffness / (stiffness + right_side), 1.0)]
    return jnp.stack(weights, 2).astype(jnp.float32)


def draw_front_inverse(key, part):
    interface = 4 * FACE_DOFS
    shape_all = (N_SUB, N_COARSE, interface, interface)
    noise = jax.random.normal(jax.random.fold_in(key, 31), shape_all, jnp.float32)
    diagonal = (lax.broadcasted_iota(jnp.int32, (interface, interface), 0) == lax.broadcasted_iota(jnp.int32, (interface, interface), 1)).astype(jnp.float32)
    return (noise * (0.6 / math.sqrt(interface)) + diagonal).astype(jnp.bfloat16)


def draw_coarse_inverse(key, part):
    line_order = N_COARSE * VERTEX_COUNT
    shape_all = (N_SUB, line_order, line_order)
    noise = jax.random.normal(jax.random.fold_in(key, 41), shape_all, jnp.float32)
    symmetric = (noise + jnp.swapaxes(noise, 1, 2)) * (0.35 / math.sqrt(line_order))
    diagonal = (lax.broadcasted_iota(jnp.int32, (line_order, line_order), 0) == lax.broadcasted_iota(jnp.int32, (line_order, line_order), 1)).astype(jnp.float32)
    return (symmetric + diagonal).astype(jnp.bfloat16)


def draw_chain_transfer(key, part):
    share_slow = 0.5
    slow_mask = jax.random.bernoulli(jax.random.fold_in(key, 21), share_slow, (CHANNELS,))
    slow_rate = jnp.exp(-jax.random.uniform(jax.random.fold_in(key, 22), (N_SUB, CHANNELS), jnp.float32, 0.2, 1.5) / N_SUB)
    fast_rate = jnp.exp(-jax.random.uniform(jax.random.fold_in(key, 23), (N_SUB, CHANNELS), jnp.float32, 1.0, 3.0))
    cooling_speeds = jnp.where(slow_mask[None, :], slow_rate, fast_rate)
    cooling_pulses = jax.random.bernoulli(jax.random.fold_in(key, 24), 3.0 / N_SUB, (N_SUB, 1))
    cooling_speeds = cooling_speeds * jnp.where(cooling_pulses, 0.6, 1.0)
    mixing = jax.random.normal(jax.random.fold_in(key, 25), (N_SUB, CHANNELS, CHANNELS), jnp.float32) * (0.2 / math.sqrt(CHANNELS))
    diagonal = (lax.broadcasted_iota(jnp.int32, (CHANNELS, CHANNELS), 0) == lax.broadcasted_iota(jnp.int32, (CHANNELS, CHANNELS), 1)).astype(jnp.float32)
    return mixing + diagonal[None] * cooling_speeds[:, :, None]


def levels(stream_key, shape, shards, low, high):
    level, own = 1.0, jax.random.fold_in(stream_key, 6)
    for axis_at, parts in shards:
        steps = jnp.exp(jax.random.uniform(jax.random.fold_in(own, axis_at), (parts,), jnp.float32, low / len(shards), high / len(shards)))
        level = level * jnp.repeat(steps, shape[axis_at] // parts).reshape([-1 if axis == axis_at else 1 for axis in range(len(shape))])
    return level


def choose_distinct(key, rows, number_of, top, lift):
    sequence = jax.random.permutation(jax.random.fold_in(key, 1), number_of)
    pull = sequence
    for power in range(3):
        pull = pull * pull // number_of
    pull = pull * lift // number_of
    chance = jax.random.randint(jax.random.fold_in(key, 2), (rows, number_of), 0, 4096) + pull
    sure = jax.random.permutation(jax.random.fold_in(key, 3), rows)[jnp.arange(number_of) % rows]
    chance = jnp.where(jnp.arange(rows)[:, None] == sure[None, :], 1 << 14, chance)
    score = chance * number_of + jnp.arange(number_of)
    return lax.top_k(score.astype(jnp.int32), top)[1].astype(jnp.int32)


def scatter_about(own_key, shape, scale, reach, cuts=(), dtype=jnp.bfloat16):
    array = scale * jax.random.normal(own_key, shape, jnp.float32)
    if cuts:
        array = array * levels(own_key, shape, cuts, -0.22, 0.18)
    return jnp.clip(array, -reach, reach).astype(dtype)


def setup_inputs(seed: int = 0) -> dict:
    arg_keys = jax.random.split(jax.random.key(seed), 12)
    residual_parts = scatter_about(arg_keys[0], (N_SUB, N_COARSE, 4, SAMPLES, FACE_DOFS), 1.0, 6.0, ((0, 16), (1, 2)))
    face_slot = jax.vmap(lambda own: jax.random.permutation(own, 4))(jax.random.split(arg_keys[1], N_SUB * N_COARSE)).reshape((N_SUB, N_COARSE, 4)).astype(jnp.int32)
    face_order = jax.vmap(lambda own: jax.random.permutation(own, FACE_DOFS))(jax.random.split(arg_keys[2], N_SUB * N_COARSE * 4)).reshape((N_SUB, N_COARSE, 4, FACE_DOFS)).astype(jnp.int32)
    face_scale = draw_face_scale(jax.random.fold_in(arg_keys[11], 71), 0)
    vertex_unknowns = choose_distinct(arg_keys[4], N_SUB * N_COARSE, 4 * FACE_DOFS, VERTEX_COUNT, 0).reshape((N_SUB, N_COARSE, VERTEX_COUNT))
    front_inverse = draw_front_inverse(jax.random.fold_in(arg_keys[11], 71), 0)
    coarse_basis = scatter_about(arg_keys[6], (N_SUB, N_COARSE, 4 * FACE_DOFS, VERTEX_COUNT), (4 * FACE_DOFS) ** -0.5, 0.125, ((0, 16), (1, 2)))
    coarse_inverse = draw_coarse_inverse(jax.random.fold_in(arg_keys[11], 71), 0)
    thermal_handoff = scatter_about(arg_keys[8], (N_SUB, N_COARSE * VERTEX_COUNT, CHANNELS), (N_COARSE * VERTEX_COUNT) ** -0.5, 0.25, ((0, 16),))
    chain_transfer = draw_chain_transfer(jax.random.fold_in(arg_keys[11], 71), 0)
    coupling_in = scatter_about(arg_keys[10], (N_SUB, CHANNELS, N_COARSE * VERTEX_COUNT), CHANNELS ** -0.5, 0.5, ((0, 16), (2, 2)))
    return dict(residual_parts=residual_parts, face_slot=face_slot, face_order=face_order, face_scale=face_scale, vertex_unknowns=vertex_unknowns, front_inverse=front_inverse, coarse_basis=coarse_basis, coarse_inverse=coarse_inverse, thermal_handoff=thermal_handoff, chain_transfer=chain_transfer, coupling_in=coupling_in)


HIGHEST = lax.Precision.HIGHEST


def canonical(values, face_slot, face_order):
    ordered = jnp.take_along_axis(values, face_order[:, :, :, None, :], axis=4)
    return jnp.take_along_axis(ordered, face_slot[:, :, :, None, None], axis=2)


def restore_layout(values, face_slot, face_order):
    slot_back = jnp.argsort(face_slot, axis=2)
    order_back = jnp.argsort(face_order, axis=3)
    by_face = jnp.take_along_axis(values, slot_back[:, :, :, None, None], axis=2)
    return jnp.take_along_axis(by_face, order_back[:, :, :, None, :], axis=4)


def neighbours(values):
    zero_sub = jnp.zeros_like(values[:1, :, 0])
    from_lower = jnp.concatenate([zero_sub, values[:-1, :, 1]], 0)
    from_upper = jnp.concatenate([values[1:, :, 0], zero_sub], 0)
    zero_across = jnp.zeros_like(values[:, :1, 2])
    from_left = jnp.concatenate([zero_across, values[:, :-1, 3]], 1)
    from_right = jnp.concatenate([values[:, 1:, 2], zero_across], 1)
    return jnp.stack([from_lower, from_upper, from_left, from_right], 2)


def reference(residual_parts, face_slot, face_order, face_scale, vertex_unknowns, front_inverse, coarse_basis, coarse_inverse, thermal_handoff, chain_transfer, coupling_in):
    scale_grid = face_scale[:, :, :, None, None]
    canon = canonical(residual_parts, face_slot, face_order)
    averaged = (scale_grid * (canon.astype(jnp.float32) + neighbours(canon).astype(jnp.float32))).astype(jnp.bfloat16)
    local_residual = restore_layout(averaged, face_slot, face_order)
    sub_rows, sub_cols, face_count, sample_count, block_size = residual_parts.shape
    subdomains = sub_rows * sub_cols
    flat_residual = local_residual.reshape(subdomains, face_count, sample_count, block_size)
    flat_inverse = front_inverse.reshape(subdomains, face_count, block_size, face_count, block_size)
    flat_basis = coarse_basis.reshape(subdomains, face_count, block_size, -1)
    vertex_vector = vertex_unknowns.reshape(subdomains, -1)

    def local_work(items):
        residual, inverse, basis, primal_values = items
        positions = lax.broadcasted_iota(jnp.int32, (primal_values.shape[0], face_count * block_size), 1)
        hits = jnp.sum((primal_values[:, None] == positions).astype(jnp.int32), axis=0)
        dual_mask = (1 - hits).astype(jnp.bfloat16).reshape(face_count, 1, block_size)
        masked = (residual * dual_mask).astype(jnp.float32)
        dual = jnp.einsum("gnj,gjfk->fnk", masked, inverse.astype(jnp.float32), precision=HIGHEST) * dual_mask.astype(jnp.float32)
        wide_space = jnp.einsum("gnj,gjc->nc", residual.astype(jnp.float32), basis.astype(jnp.float32), precision=HIGHEST).astype(jnp.bfloat16)
        return dual, wide_space

    dual_part, coarse_residual = lax.map(local_work, (flat_residual, flat_inverse, flat_basis, vertex_vector))
    primal_count = coarse_residual.shape[-1]
    residual_of_line = coarse_residual.reshape(sub_rows, sub_cols, sample_count, primal_count).transpose(0, 2, 1, 3).reshape(sub_rows, sample_count, sub_cols * primal_count)
    line_base = jnp.einsum("pnl,plm->pnm", residual_of_line.astype(jnp.float32), coarse_inverse.astype(jnp.float32), precision=HIGHEST)
    inflow = jnp.einsum("pnl,plk->pnk", residual_of_line.astype(jnp.float32), thermal_handoff.astype(jnp.float32), precision=HIGHEST)

    def carry_step(state_now, items):
        transfer, incoming = items
        return jnp.dot(state_now, transfer, precision=HIGHEST) + incoming, state_now

    final_state, carried = lax.scan(carry_step, jnp.zeros_like(inflow[0]), (chain_transfer, inflow))
    line_solution = (line_base + jnp.einsum("pnk,pkm->pnm", carried, coupling_in.astype(jnp.float32), precision=HIGHEST)).astype(jnp.bfloat16)
    own_coarse = line_solution.reshape(sub_rows, sample_count, sub_cols, primal_count).transpose(0, 2, 1, 3).reshape(subdomains, sample_count, primal_count)

    def extend_to_faces(items):
        wide_space, basis = items
        return jnp.einsum("nc,gjc->gnj", wide_space.astype(jnp.float32), basis.astype(jnp.float32), precision=HIGHEST)

    coarse_part = lax.map(extend_to_faces, (own_coarse, flat_basis))
    subregion_iterate = (dual_part + coarse_part).reshape(sub_rows, sub_cols, face_count, sample_count, block_size)
    weighted = (scale_grid * canonical(subregion_iterate, face_slot, face_order)).astype(jnp.bfloat16)
    summed = (weighted.astype(jnp.float32) + neighbours(weighted).astype(jnp.float32)).astype(jnp.bfloat16)
    return restore_layout(summed, face_slot, face_order)
```

```python
import jax
import jax.numpy as jnp
from jax import lax
from jax.sharding import PartitionSpec as P

HIGHEST = lax.Precision.HIGHEST


def one_hot_rows(order, count):
    return (
        order[:, None, :] == lax.broadcasted_iota(jnp.int32, (order.shape[0], count, order.shape[1]), 1)
    ).astype(jnp.bfloat16)


def shifted(array, axis, step):
    count = lax.axis_size(axis)
    pairs = [(i, i + step) for i in range(count) if 0 <= i + step < count]
    return lax.ppermute(array, axis, pairs)


def trade(by_direction):
    return [
        shifted(by_direction[1], "sub", 1),
        shifted(by_direction[0], "sub", -1),
        shifted(by_direction[3], "coarse", 1),
        shifted(by_direction[2], "coarse", -1),
    ]


def per_device(
    residual_parts,
    face_slot,
    face_order,
    face_scale,
    vertex_unknowns,
    front_inverse,
    coarse_basis,
    coarse_inverse,
    thermal_handoff,
    chain_transfer,
    coupling_in,
):
    f32, bf16 = jnp.float32, jnp.bfloat16
    parts = residual_parts[0, 0]
    slot = face_slot[0, 0]
    scale = face_scale[0, 0]
    face_count, sample_count, block_size = parts.shape
    by_slot = jnp.argsort(slot)
    order = face_order[0, 0]
    own_canon_order = jnp.stack([order[slot[d]] for d in range(4)])
    own_faces = [parts[slot[d]] for d in range(4)]
    transfer = chain_transfer[0]
    peers, mine = lax.axis_size("sub"), lax.axis_index("sub")
    transfers = lax.all_gather(transfer, "sub")
    their_orders = jnp.stack(trade([own_canon_order[d] for d in range(4)]))
    theirs = trade(own_faces)
    own_table = one_hot_rows(own_canon_order, block_size)
    high, low = (their_orders >> 4).astype(bf16), (their_orders & 15).astype(bf16)
    comp = jnp.einsum("dxj,dkj->dxk", jnp.stack([high, low], 1), own_table, preferred_element_type=f32)
    comp = (comp[:, 0] * 16 + comp[:, 1]).astype(jnp.int32)
    tables = one_hot_rows(comp, block_size)
    rows = [scale[d] * (
        own_faces[d].astype(f32)
        + jnp.dot(theirs[d], tables[d], preferred_element_type=f32)
    ) for d in range(4)]
    averaged = [row.astype(bf16) for row in rows]
    local_residual = jnp.stack(averaged)[by_slot]
    own_primal = vertex_unknowns[0, 0]
    positions = lax.broadcasted_iota(jnp.int32, (own_primal.shape[0], face_count * block_size), 1)
    hits = jnp.sum((own_primal[:, None] == positions).astype(jnp.int32), axis=0)
    dual_mask = (1 - hits).astype(bf16)
    flat = local_residual.transpose(1, 0, 2).reshape(sample_count, face_count * block_size)
    basis = coarse_basis[0, 0]
    coarse_residual = jnp.dot(flat, basis, preferred_element_type=f32).astype(bf16)
    primal_count = coarse_residual.shape[1]
    own_rows = lax.dynamic_slice_in_dim(
        thermal_handoff[0], lax.axis_index("coarse") * primal_count, primal_count, 0
    )
    line_residual = lax.all_gather(coarse_residual, "coarse", axis=1, tiled=True)
    inflow = jnp.dot(line_residual, thermal_handoff[0], preferred_element_type=f32)
    inflows = lax.all_gather(inflow.astype(bf16), "sub")
    dual_part = jnp.dot(flat * dual_mask, front_inverse[0, 0], preferred_element_type=f32) * dual_mask.astype(f32)
    channels = transfer.shape[0]
    eye = jnp.eye(channels, dtype=f32)
    index = lax.broadcasted_iota(jnp.int32, (peers, 1, 1), 0)
    chain = jnp.where(index < mine, transfers, eye)
    step = 1
    while step < peers:
        later = jnp.concatenate([chain[step:], jnp.broadcast_to(eye, (step, channels, channels))], 0)
        chain = jnp.einsum("pab,pbc->pac", chain, later, precision=HIGHEST)
        step *= 2
    weights = jnp.concatenate([chain[1:], eye[None]], 0)
    weights = jnp.where(index < mine, weights, 0.0).astype(bf16)
    carried = jnp.einsum("pna,pac->nc", inflows, weights, preferred_element_type=f32)
    line_base = jnp.dot(line_residual, coarse_inverse[0], preferred_element_type=f32)
    answer = (line_base + jnp.dot(carried.astype(bf16), coupling_in[0], preferred_element_type=f32)).astype(bf16)
    iterate = dual_part + lax.dot_general(
        answer, basis, (((1,), (1,)), ((), ())), preferred_element_type=f32
    )
    iterate = iterate.reshape(sample_count, face_count, block_size).transpose(1, 0, 2)
    weighted = (scale[by_slot][:, None, None] * iterate).astype(bf16)
    weighted_d = [weighted[slot[d]] for d in range(4)]
    theirs = trade(weighted_d)
    summed = jnp.stack([
        (weighted_d[d].astype(f32) + jnp.dot(theirs[d], tables[d], preferred_element_type=f32)).astype(bf16)
        for d in range(4)
    ])
    return summed[by_slot][None, None]


def solution(mesh):
    placed = (
        P("sub", "coarse", None, None, None),
        P("sub", "coarse", None),
        P("sub", "coarse", None, None),
        P("sub", "coarse", None),
        P("sub", "coarse", None),
        P("sub", "coarse", None, None),
        P("sub", "coarse", None, None),
        P("sub", None, "coarse"),
        P("sub", None, None),
        P("sub", None, None),
        P("sub", None, "coarse"),
    )
    return jax.shard_map(
        per_device,
        mesh=mesh,
        in_specs=placed,
        out_specs=P("sub", "coarse", None, None, None),
        check_vma=False,
    )
```

```python
import functools

import jax
import jax.numpy as jnp
from jax import lax
from jax.experimental import pallas as pl
from jax.experimental.pallas import tpu as pltpu
from jax.sharding import PartitionSpec as P

MESH = pl.DeviceIdType.MESH
F32, BF16 = jnp.float32, jnp.bfloat16
NT = (((1,), (1,)), ((), ()))


def dot(a, b):
    return jnp.dot(a, b, preferred_element_type=F32)


def dot_nt(a, b):
    return lax.dot_general(a, b, NT, preferred_element_type=F32)


def split_rows(x):
    high = x.astype(BF16).astype(F32)
    return jnp.concatenate([high, x - high], axis=0).astype(BF16)


def kernel(
    peers,
    lines,
    slot_ref,
    scale_ref,
    parts_ref,
    order_ref,
    primal_ref,
    transfer_ref,
    inverse_hbm,
    basis_hbm,
    line_hbm,
    handoff_hbm,
    coupling_hbm,
    out_ref,
    inverse,
    basis,
    line,
    handoff,
    coupling,
    face_out,
    face_in,
    order_out,
    order_in,
    table,
    placed,
    residual,
    dual,
    mask,
    coarse,
    transfers,
    inflow,
    heat_in,
    heat_out,
    carried,
    weighted,
    face_out2,
    face_in2,
    load_sem,
    face_send,
    face_recv,
    order_send,
    order_recv,
    coarse_send,
    coarse_recv,
    chip_send,
    chip_recv,
    core_send,
    core_recv,
    heat_send,
    heat_recv,
    back_send,
    back_recv,
    face_send2,
    face_recv2,
):
    me, col = lax.axis_index("sub"), lax.axis_index("coarse")
    faces, samples, block = parts_ref.shape
    primal = basis.shape[1]
    rows = samples // peers
    chips = peers // 2
    chip, core = me // 2, lax.rem(me, 2)

    loads = [
        pltpu.make_async_copy(source, target, load_sem.at[i])
        for i, (source, target) in enumerate(
            [
                (basis_hbm, basis),
                (inverse_hbm, inverse),
                (handoff_hbm, handoff),
                (line_hbm, line),
                (coupling_hbm, coupling),
            ]
        )
    ]
    for load in loads:
        load.start()

    barrier = pltpu.get_barrier_semaphore()

    @pl.loop(1, peers)
    def _(k):
        pl.semaphore_signal(
            barrier, inc=1, device_id=(lax.rem(me + k, peers), col), device_id_type=MESH
        )

    @pl.loop(1, lines)
    def _(k):
        pl.semaphore_signal(
            barrier, inc=1, device_id=(me, lax.rem(col + k, lines)), device_id_type=MESH
        )

    slots = [slot_ref[d] for d in range(4)]
    direction = []
    for s in range(4):
        found = jnp.int32(0)
        for d in range(1, 4):
            found = jnp.where(slots[d] == s, d, found)
        direction.append(found)
    scales = [scale_ref[direction[s]] for s in range(4)]

    for d in range(4):
        face_out[d] = parts_ref[slots[d]]
        own = order_ref[pl.ds(slots[d], 1), :]
        order_out[d] = jnp.broadcast_to(own, (8, block))
    transfers[core, chip] = transfer_ref[...].astype(BF16)

    pl.semaphore_wait(barrier, peers - 1 + lines - 1)

    exists = [me > 0, me < peers - 1, col > 0, col < lines - 1]
    beside = [
        (jnp.maximum(me - 1, 0), col),
        (jnp.minimum(me + 1, peers - 1), col),
        (me, jnp.maximum(col - 1, 0)),
        (me, jnp.minimum(col + 1, lines - 1)),
    ]

    def face_copy(source, target, send, recv, d, at):
        return pltpu.make_async_remote_copy(
            src_ref=source.at[d],
            dst_ref=target.at[at],
            send_sem=send.at[d],
            recv_sem=recv.at[at],
            device_id=beside[d],
            device_id_type=MESH,
        )

    def orders(d, at):
        return face_copy(order_out, order_in, order_send, order_recv, d, at)

    def first(d, at):
        return face_copy(face_out, face_in, face_send, face_recv, d, at)

    def second(d, at):
        return face_copy(face_out2, face_in2, face_send2, face_recv2, d, at)

    for d in (2, 3, 0, 1):

        @pl.when(exists[d])
        def _():
            orders(d, d ^ 1).start()
            first(d, d ^ 1).start()

    def to_chip(target, source):
        return pltpu.make_async_remote_copy(
            src_ref=transfers.at[core, source],
            dst_ref=transfers.at[core, source],
            send_sem=chip_send.at[target],
            recv_sem=chip_recv.at[source],
            device_id=(target * 2 + core, col),
            device_id_type=MESH,
        )

    @pl.loop(1, chips)
    def _(k):
        to_chip(lax.rem(chip + k, chips), chip).start()

    ids = primal_ref[...]
    count = ids.shape[1]
    groups = faces * block // 128
    group_hit = jnp.where(lax.broadcasted_iota(jnp.int32, (groups, count), 0) == ids // 128, 1.0, 0.0)
    lane_hit = jnp.where(lax.broadcasted_iota(jnp.int32, (128, count), 0) == ids % 128, 1.0, 0.0)
    kept = 1.0 - dot_nt(group_hit.astype(BF16), lane_hit.astype(BF16))
    per_face = block // 128
    for s in range(4):
        row = jnp.concatenate(
            [kept[s * per_face + t : s * per_face + t + 1] for t in range(per_face)], axis=1
        )
        mask[s] = jnp.broadcast_to(row, (8, block))

    for d in (0, 1, 2, 3):

        @pl.when(exists[d])
        def _():
            position = lax.broadcasted_iota(jnp.int32, (block, block), 0)
            own_table = jnp.where(position == order_out[d, 0:1, :], 1.0, 0.0).astype(BF16)
            orders(d, d).wait_recv()
            theirs = order_in[d]
            halves = jnp.concatenate([theirs // 16, theirs % 16], axis=0)
            found = dot_nt(halves.astype(F32).astype(BF16), own_table)
            joined = (found[0:1] * 16.0 + found[8:9]).astype(jnp.int32)
            table[d] = jnp.where(position == joined, 1.0, 0.0).astype(BF16)

    def place(d, copy, landed):
        @pl.when(exists[d])
        def _():
            copy(d, d).wait_recv()
            placed[d] = dot(landed[d], table[d]).astype(BF16)

        @pl.when(jnp.logical_not(exists[d]))
        def _():
            placed[d] = jnp.zeros((samples, block), BF16)

    for d in (0, 1, 2, 3):
        place(d, first, face_in)
    for s in range(4):
        total = parts_ref[s].astype(F32) + placed[direction[s]].astype(F32)
        residual[:, s * block : (s + 1) * block] = (scales[s] * total).astype(BF16)

    loads[0].wait()
    own_coarse = dot(residual[...], basis[...])
    coarse[col] = own_coarse.astype(BF16)

    def to_line(target, source):
        return pltpu.make_async_remote_copy(
            src_ref=coarse.at[source],
            dst_ref=coarse.at[source],
            send_sem=coarse_send.at[target],
            recv_sem=coarse_recv.at[source],
            device_id=(me, target),
            device_id_type=MESH,
        )

    @pl.loop(1, lines)
    def _(k):
        to_line(lax.rem(col + k, lines), col).start()

    @pl.loop(1, chips)
    def _(k):
        to_chip(chip, lax.rem(chip + k, chips)).wait_recv()

    def to_core(which):
        return pltpu.make_async_remote_copy(
            src_ref=transfers.at[which],
            dst_ref=transfers.at[which],
            send_sem=core_send,
            recv_sem=core_recv,
            device_id=(chip * 2 + 1 - core, col),
            device_id_type=MESH,
        )

    to_core(core).start()

    for s in range(4):
        at = slice(s * block, (s + 1) * block)
        residual[:, at] = (residual[:, at].astype(F32) * mask[s, 0:1, :]).astype(BF16)
    loads[1].wait()

    @pl.loop(0, 4)
    def _(s):
        at = pl.ds(pl.multiple_of(s * block, block), block)
        dual[s] = dot(residual[...], inverse[:, at]) * mask[s, 0:1, :]

    loads[2].wait()

    @pl.loop(1, lines)
    def _(k):
        to_line(col, lax.rem(col + k, lines)).wait_recv()

    heat = jnp.zeros((samples, handoff.shape[1]), F32)
    for q in range(lines):
        heat += dot(coarse[q], handoff[q * primal : (q + 1) * primal, :])
    inflow[...] = heat

    def to_samples(target, source):
        return pltpu.make_async_remote_copy(
            src_ref=inflow.at[pl.ds(pl.multiple_of(target * rows, rows), rows)],
            dst_ref=heat_in.at[source],
            send_sem=heat_send.at[target],
            recv_sem=heat_recv.at[source],
            device_id=(target, col),
            device_id_type=MESH,
        )

    @pl.loop(1, peers)
    def _(k):
        to_samples(lax.rem(me + k, peers), me).start()

    heat_in[me] = inflow[pl.ds(pl.multiple_of(me * rows, rows), rows), :]

    loads[3].wait()
    base = jnp.zeros((samples, primal), F32)
    for q in range(lines):
        base += dot(coarse[q], line[q * primal : (q + 1) * primal, :])

    to_core(1 - core).wait_recv()

    def to_lines(target, source):
        return pltpu.make_async_remote_copy(
            src_ref=heat_out.at[target],
            dst_ref=carried.at[pl.ds(pl.multiple_of(source * rows, rows), rows)],
            send_sem=back_send.at[target],
            recv_sem=back_recv.at[source],
            device_id=(target, col),
            device_id_type=MESH,
        )

    def advance(p, state):
        heat_out[p] = state

        @pl.when(p != me)
        def _():
            to_lines(p, me).start()
            to_samples(me, p).wait_recv()

        split = dot(split_rows(state), transfers[lax.rem(p, 2), p // 2])
        return split[:rows] + split[rows:] + heat_in[p]

    lax.fori_loop(0, peers, advance, jnp.zeros((rows, handoff.shape[1]), F32))
    carried[pl.ds(pl.multiple_of(me * rows, rows), rows), :] = heat_out[me]
    loads[4].wait()

    @pl.loop(1, peers)
    def _(k):
        to_lines(me, lax.rem(me + k, peers)).wait_recv()

    coupled = dot(split_rows(carried[...]), coupling[...])
    answer = (base + coupled[:samples] + coupled[samples:]).astype(BF16)
    for s in range(4):
        found = dual[s] + dot_nt(answer, basis[s * block : (s + 1) * block, :])
        weighted[s] = (scales[s] * found).astype(BF16)
    for d in (2, 3, 0, 1):
        face_out2[d] = weighted[slots[d]]

        @pl.when(exists[d])
        def _():
            second(d, d ^ 1).start()

    for d in (0, 1, 2, 3):
        place(d, second, face_in2)
    for s in range(4):
        total = weighted[s].astype(F32) + placed[direction[s]].astype(F32)
        out_ref[s] = total.astype(BF16)

    for d in range(4):

        @pl.when(exists[d])
        def _():
            orders(d, d ^ 1).wait_send()
            first(d, d ^ 1).wait_send()
            second(d, d ^ 1).wait_send()

    @pl.loop(1, chips)
    def _(k):
        to_chip(lax.rem(chip + k, chips), chip).wait_send()

    to_core(core).wait_send()

    @pl.loop(1, lines)
    def _(k):
        to_line(lax.rem(col + k, lines), col).wait_send()

    @pl.loop(1, peers)
    def _(k):
        to_samples(lax.rem(me + k, peers), me).wait_send()
        to_lines(lax.rem(me + k, peers), me).wait_send()


def per_device(
    peers,
    lines,
    residual_parts,
    face_slot,
    face_order,
    face_scale,
    vertex_unknowns,
    front_inverse,
    coarse_basis,
    coarse_inverse,
    thermal_handoff,
    chain_transfer,
    coupling_in,
):
    faces, samples, block = residual_parts.shape[2:]
    interface = faces * block
    primal = coarse_basis.shape[-1]
    channels = chain_transfer.shape[-1]
    rows = samples // peers
    dma = pltpu.SemaphoreType.DMA
    vmem, smem, hbm = (
        pl.BlockSpec(memory_space=space) for space in (pltpu.VMEM, pltpu.SMEM, pl.ANY)
    )
    stack = pltpu.VMEM((faces, samples, block), BF16)
    out = pl.pallas_call(
        functools.partial(kernel, peers, lines),
        out_shape=jax.ShapeDtypeStruct((faces, samples, block), BF16),
        in_specs=[smem] * 2 + [vmem] * 4 + [hbm] * 5,
        out_specs=vmem,
        scratch_shapes=[
            pltpu.VMEM((interface, interface), BF16),
            pltpu.VMEM((interface, primal), BF16),
            pltpu.VMEM((lines * primal, primal), BF16),
            pltpu.VMEM((lines * primal, channels), BF16),
            pltpu.VMEM((channels, primal), BF16),
            stack,
            stack,
            pltpu.VMEM((faces, 8, block), jnp.int32),
            pltpu.VMEM((faces, 8, block), jnp.int32),
            pltpu.VMEM((faces, block, block), BF16),
            stack,
            pltpu.VMEM((samples, interface), BF16),
            pltpu.VMEM((faces, samples, block), F32),
            pltpu.VMEM((faces, 8, block), F32),
            pltpu.VMEM((lines, samples, primal), BF16),
            pltpu.VMEM((2, peers // 2, channels, channels), BF16),
            pltpu.VMEM((samples, channels), F32),
            pltpu.VMEM((peers, rows, channels), F32),
            pltpu.VMEM((peers, rows, channels), F32),
            pltpu.VMEM((samples, channels), F32),
            stack,
            stack,
            stack,
            dma((5,)),
            dma((4,)),
            dma((4,)),
            dma((4,)),
            dma((4,)),
            dma((lines,)),
            dma((lines,)),
            dma((peers // 2,)),
            dma((peers // 2,)),
            dma,
            dma,
            dma((peers,)),
            dma((peers,)),
            dma((peers,)),
            dma((peers,)),
            dma((4,)),
            dma((4,)),
        ],
        compiler_params=pltpu.CompilerParams(
            collective_id=0, has_side_effects=True, vmem_limit_bytes=48 * 1024 * 1024
        ),
    )(
        face_slot[0, 0],
        face_scale[0, 0],
        residual_parts[0, 0],
        face_order[0, 0],
        vertex_unknowns[0],
        chain_transfer[0],
        front_inverse[0, 0],
        coarse_basis[0, 0],
        coarse_inverse[0],
        thermal_handoff[0],
        coupling_in[0],
    )
    return out[None, None]


def solution(mesh):
    placed = (
        P("sub", "coarse", None, None, None),
        P("sub", "coarse", None),
        P("sub", "coarse", None, None),
        P("sub", "coarse", None),
        P("sub", "coarse", None),
        P("sub", "coarse", None, None),
        P("sub", "coarse", None, None),
        P("sub", None, "coarse"),
        P("sub", None, None),
        P("sub", None, None),
        P("sub", None, "coarse"),
    )
    return jax.shard_map(
        functools.partial(per_device, mesh.shape["sub"], mesh.shape["coarse"]),
        mesh=mesh,
        in_specs=placed,
        out_specs=P("sub", "coarse", None, None, None),
        check_vma=False,
    )
```

```python
import functools

import jax
import jax.numpy as jnp
from jax import lax
from jax.experimental import pallas as pl
from jax.experimental.pallas import tpu as pltpu
from jax.sharding import PartitionSpec as P

MESH = pl.DeviceIdType.MESH
F32, BF16 = jnp.float32, jnp.bfloat16
NT = (((1,), (1,)), ((), ()))


def dot(a, b):
    return jnp.dot(a, b, preferred_element_type=F32)


def dot_nt(a, b):
    return lax.dot_general(a, b, NT, preferred_element_type=F32)


def split_rows(x):
    high = x.astype(BF16).astype(F32)
    return jnp.concatenate([high, x - high], axis=0).astype(BF16)


def shares(samples, peers, lines):
    rows = samples // peers
    return lines if rows % (8 * lines) == 0 else 1


def kernel(
    peers,
    lines,
    slot_hbm,
    scale_hbm,
    parts_hbm,
    order_hbm,
    primal_hbm,
    transfer_hbm,
    inverse_hbm,
    basis_hbm,
    line_hbm,
    handoff_hbm,
    coupling_hbm,
    out_ref,
    slot_ref,
    scale_ref,
    parts_ref,
    order_ref,
    primal_ref,
    transfer_ref,
    inverse,
    basis,
    line,
    handoff,
    coupling,
    face_out,
    face_in,
    order_out,
    order_in,
    table,
    placed,
    residual,
    dual,
    mask,
    coarse,
    transfers,
    within,
    through,
    inflow,
    heat_in,
    heat_out,
    carried,
    weighted,
    face_out2,
    face_in2,
    load_sem,
    face_send,
    face_recv,
    order_send,
    order_recv,
    coarse_send,
    coarse_recv,
    chip_send,
    chip_recv,
    core_send,
    core_recv,
    heat_send,
    heat_recv,
    back_send,
    back_recv,
    face_send2,
    face_recv2,
):
    me, col = lax.axis_index("sub"), lax.axis_index("coarse")
    faces, samples, block = parts_ref.shape
    primal = basis.shape[1]
    share = shares(samples, peers, lines)
    rows = samples // (peers * share)
    chips = peers // 2
    chip, core = me // 2, lax.rem(me, 2)

    loads = [
        pltpu.make_async_copy(source, target, load_sem.at[i])
        for i, (source, target) in enumerate(
            [
                (slot_hbm, slot_ref),
                (scale_hbm, scale_ref),
                (parts_hbm, parts_ref),
                (order_hbm, order_ref),
                (transfer_hbm, transfer_ref),
                (primal_hbm, primal_ref),
                (basis_hbm, basis),
                (handoff_hbm, handoff),
                (inverse_hbm, inverse),
                (line_hbm, line),
                (coupling_hbm, coupling),
            ]
        )
    ]
    for load in loads:
        load.start()

    barrier = pltpu.get_barrier_semaphore()

    def other(n):
        return lax.rem(me + lax.rem(n, peers), peers), lax.rem(col + n // peers, lines)

    @pl.loop(1, peers * share)
    def _(n):
        pl.semaphore_signal(barrier, inc=1, device_id=other(n), device_id_type=MESH)

    if share == 1:

        @pl.loop(1, lines)
        def _(k):
            pl.semaphore_signal(
                barrier, inc=1, device_id=(me, lax.rem(col + k, lines)), device_id_type=MESH
            )

    for load in loads[:5]:
        load.wait()
    slots = [slot_ref[d] for d in range(4)]
    direction = []
    for s in range(4):
        found = jnp.int32(0)
        for d in range(1, 4):
            found = jnp.where(slots[d] == s, d, found)
        direction.append(found)
    scales = [scale_ref[direction[s]] for s in range(4)]

    for d in range(4):
        face_out[d] = parts_ref[slots[d]]
        own = order_ref[pl.ds(slots[d], 1), :]
        order_out[d] = jnp.broadcast_to(own, (8, block))
    transfers[core, chip] = transfer_ref[...].astype(BF16)

    pl.semaphore_wait(barrier, peers * share - 1 + (lines - 1 if share == 1 else 0))

    exists = [me > 0, me < peers - 1, col > 0, col < lines - 1]
    beside = [
        (jnp.maximum(me - 1, 0), col),
        (jnp.minimum(me + 1, peers - 1), col),
        (me, jnp.maximum(col - 1, 0)),
        (me, jnp.minimum(col + 1, lines - 1)),
    ]

    def face_copy(source, target, send, recv, d, at):
        return pltpu.make_async_remote_copy(
            src_ref=source.at[d],
            dst_ref=target.at[at],
            send_sem=send.at[d],
            recv_sem=recv.at[at],
            device_id=beside[d],
            device_id_type=MESH,
        )

    def orders(d, at):
        return face_copy(order_out, order_in, order_send, order_recv, d, at)

    def first(d, at):
        return face_copy(face_out, face_in, face_send, face_recv, d, at)

    def second(d, at):
        return face_copy(face_out2, face_in2, face_send2, face_recv2, d, at)

    for d in (2, 3, 0, 1):

        @pl.when(exists[d])
        def _():
            orders(d, d ^ 1).start()
            first(d, d ^ 1).start()

    def to_chip(target, source):
        return pltpu.make_async_remote_copy(
            src_ref=transfers.at[core, source],
            dst_ref=transfers.at[core, source],
            send_sem=chip_send.at[target],
            recv_sem=chip_recv.at[source],
            device_id=(target * 2 + core, col),
            device_id_type=MESH,
        )

    @pl.loop(1, chips)
    def _(k):
        to_chip(lax.rem(chip + k, chips), chip).start()

    loads[5].wait()
    ids = primal_ref[...]
    count = ids.shape[1]
    groups = faces * block // 128
    group_hit = jnp.where(lax.broadcasted_iota(jnp.int32, (groups, count), 0) == ids // 128, 1.0, 0.0)
    lane_hit = jnp.where(lax.broadcasted_iota(jnp.int32, (128, count), 0) == ids % 128, 1.0, 0.0)
    kept = 1.0 - dot_nt(group_hit.astype(BF16), lane_hit.astype(BF16))
    per_face = block // 128
    for s in range(4):
        row = jnp.concatenate(
            [kept[s * per_face + t : s * per_face + t + 1] for t in range(per_face)], axis=1
        )
        mask[s] = jnp.broadcast_to(row, (8, block))

    for d in (0, 1, 2, 3):

        @pl.when(exists[d])
        def _():
            position = lax.broadcasted_iota(jnp.int32, (block, block), 0)
            own_table = jnp.where(position == order_out[d, 0:1, :], 1.0, 0.0).astype(BF16)
            orders(d, d).wait_recv()
            theirs = order_in[d]
            halves = jnp.concatenate([theirs // 16, theirs % 16], axis=0)
            found = dot_nt(halves.astype(F32).astype(BF16), own_table)
            joined = (found[0:1] * 16.0 + found[8:9]).astype(jnp.int32)
            table[d] = jnp.where(position == joined, 1.0, 0.0).astype(BF16)

    def place(d, copy, landed):
        @pl.when(exists[d])
        def _():
            copy(d, d).wait_recv()
            placed[d] = dot(landed[d], table[d]).astype(BF16)

        @pl.when(jnp.logical_not(exists[d]))
        def _():
            placed[d] = jnp.zeros((samples, block), BF16)

    for d in (0, 1, 2, 3):
        place(d, first, face_in)
    for s in range(4):
        total = parts_ref[s].astype(F32) + placed[direction[s]].astype(F32)
        residual[:, s * block : (s + 1) * block] = (scales[s] * total).astype(BF16)

    loads[6].wait()
    own_coarse = dot(residual[...], basis[...])
    coarse[col] = own_coarse.astype(BF16)

    def to_line(target, source):
        return pltpu.make_async_remote_copy(
            src_ref=coarse.at[source],
            dst_ref=coarse.at[source],
            send_sem=coarse_send.at[target],
            recv_sem=coarse_recv.at[source],
            device_id=(me, target),
            device_id_type=MESH,
        )

    def line_start():
        @pl.loop(1, lines)
        def _(k):
            to_line(lax.rem(col + k, lines), col).start()

    def line_wait():
        @pl.loop(1, lines)
        def _(k):
            to_line(col, lax.rem(col + k, lines)).wait_recv()

    def place_of(p, c):
        return (c if share > 1 else 0) * peers + p

    def chunk(p, c):
        first_row = (p * share + (c if share > 1 else 0)) * rows
        return pl.ds(pl.multiple_of(first_row, rows), rows)

    def to_samples(target, source):
        return pltpu.make_async_remote_copy(
            src_ref=inflow.at[chunk(*target)],
            dst_ref=heat_in.at[place_of(*source)],
            send_sem=heat_send.at[place_of(*target)],
            recv_sem=heat_recv.at[place_of(*source)],
            device_id=target,
            device_id_type=MESH,
        )

    def to_lines(target, source):
        return pltpu.make_async_remote_copy(
            src_ref=heat_out.at[target[0]],
            dst_ref=carried.at[chunk(*source)],
            send_sem=back_send.at[place_of(*target)],
            recv_sem=back_recv.at[place_of(*source)],
            device_id=target,
            device_id_type=MESH,
        )

    here = (me, col)
    loads[7].wait()
    if share > 1:
        own_rows = pl.ds(pl.multiple_of(col * primal, primal), primal)
        inflow[...] = dot(coarse[col], handoff[own_rows, :])
    else:
        line_start()
        line_wait()
        heat = jnp.zeros((samples, handoff.shape[1]), F32)
        for q in range(lines):
            heat += dot(coarse[q], handoff[q * primal : (q + 1) * primal, :])
        inflow[...] = heat

    @pl.loop(1, peers * share)
    def _(n):
        to_samples(other(n), here).start()

    if share > 1:
        line_start()
    heat_in[place_of(*here)] = inflow[chunk(*here), :]

    @pl.loop(1, chips)
    def _(k):
        to_chip(chip, lax.rem(chip + k, chips)).wait_recv()

    def to_core(which):
        return pltpu.make_async_remote_copy(
            src_ref=transfers.at[which],
            dst_ref=transfers.at[which],
            send_sem=core_send,
            recv_sem=core_recv,
            device_id=(chip * 2 + 1 - core, col),
            device_id_type=MESH,
        )

    to_core(core).start()

    for s in range(4):
        at = slice(s * block, (s + 1) * block)
        residual[:, at] = (residual[:, at].astype(F32) * mask[s, 0:1, :]).astype(BF16)
    loads[8].wait()

    def dual_face(s):
        at = pl.ds(pl.multiple_of(s * block, block), block)
        dual[s] = dot(residual[...], inverse[:, at]) * mask[s, 0:1, :]

    pl.loop(0, 2)(dual_face)

    to_core(1 - core).wait_recv()
    width = handoff.shape[1]
    groups4 = peers // 4
    nothing = jnp.zeros((width, width), BF16)
    for g in range(groups4):
        t0, t1 = transfers[0, 2 * g], transfers[1, 2 * g]
        t2, t3 = transfers[0, 2 * g + 1], transfers[1, 2 * g + 1]
        t01 = dot(t0, t1).astype(BF16)
        t12 = dot(t1, t2).astype(BF16)
        t23 = dot(t2, t3).astype(BF16)
        t012 = dot(t01, t2).astype(BF16)
        t123 = dot(t12, t3).astype(BF16)
        t0123 = dot(t012, t3).astype(BF16)
        for k, tile in enumerate((t0, t01, t012, t0123)):
            through[g, :, k * width : (k + 1) * width] = tile
        table3 = ((t1, t12, t123), (nothing, t2, t23), (nothing, nothing, t3))
        for i in range(3):
            for k in range(3):
                within[g, i * width : (i + 1) * width, k * width : (k + 1) * width] = table3[i][k]

    @pl.loop(1, peers * share)
    def _(n):
        to_samples(here, other(n)).wait_recv()

    local = []
    for g in range(groups4):
        own = []
        for i in range(4):
            total = heat_in[4 * g + i]
            for c in range(1, share):
                total = total + heat_in[c * peers + 4 * g + i]
            own.append(total)
        split = dot(split_rows(jnp.concatenate(own[:3], axis=1)), within[g])
        split = split[:rows] + split[rows:]
        local.append(
            [own[0]] + [split[:, k * width : (k + 1) * width] + own[k + 1] for k in range(3)]
        )
    state = jnp.zeros((rows, width), F32)
    for g in range(groups4):
        heat_out[4 * g] = state
        split = dot(split_rows(state), through[g])
        split = split[:rows] + split[rows:]
        ahead = [split[:, k * width : (k + 1) * width] + local[g][k] for k in range(4)]
        for k in range(3):
            heat_out[4 * g + k + 1] = ahead[k]
        state = ahead[3]

        @pl.loop(0, 4 * share)
        def _(n):
            p, c = 4 * g + lax.rem(n, 4), n // 4

            @pl.when(jnp.logical_or(p != me, c != 0))
            def _():
                to_lines((p, lax.rem(col + c, lines)), here).start()

    carried[chunk(*here), :] = heat_out[me]

    pl.loop(2, 4)(dual_face)

    if share > 1:
        line_wait()
    loads[9].wait()
    base = jnp.zeros((samples, primal), F32)
    for q in range(lines):
        base += dot(coarse[q], line[q * primal : (q + 1) * primal, :])
    loads[10].wait()

    @pl.loop(1, peers * share)
    def _(n):
        to_lines(here, other(n)).wait_recv()

    coupled = dot(split_rows(carried[...]), coupling[...])
    answer = (base + coupled[:samples] + coupled[samples:]).astype(BF16)
    for s in range(4):
        found = dual[s] + dot_nt(answer, basis[s * block : (s + 1) * block, :])
        weighted[s] = (scales[s] * found).astype(BF16)
    for d in (2, 3, 0, 1):
        face_out2[d] = weighted[slots[d]]

        @pl.when(exists[d])
        def _():
            second(d, d ^ 1).start()

    for d in (0, 1, 2, 3):
        place(d, second, face_in2)
    for s in range(4):
        total = weighted[s].astype(F32) + placed[direction[s]].astype(F32)
        out_ref[s] = total.astype(BF16)

    for d in range(4):

        @pl.when(exists[d])
        def _():
            orders(d, d ^ 1).wait_send()
            first(d, d ^ 1).wait_send()
            second(d, d ^ 1).wait_send()

    @pl.loop(1, chips)
    def _(k):
        to_chip(lax.rem(chip + k, chips), chip).wait_send()

    to_core(core).wait_send()

    @pl.loop(1, lines)
    def _(k):
        to_line(lax.rem(col + k, lines), col).wait_send()

    @pl.loop(1, peers * share)
    def _(n):
        to_samples(other(n), here).wait_send()
        to_lines(other(n), here).wait_send()


def per_device(
    peers,
    lines,
    residual_parts,
    face_slot,
    face_order,
    face_scale,
    vertex_unknowns,
    front_inverse,
    coarse_basis,
    coarse_inverse,
    thermal_handoff,
    chain_transfer,
    coupling_in,
):
    faces, samples, block = residual_parts.shape[2:]
    interface = faces * block
    primal = coarse_basis.shape[-1]
    channels = chain_transfer.shape[-1]
    share = shares(samples, peers, lines)
    rows = samples // (peers * share)
    dma = pltpu.SemaphoreType.DMA
    vmem, hbm = (pl.BlockSpec(memory_space=space) for space in (pltpu.VMEM, pltpu.HBM))
    stack = pltpu.VMEM((faces, samples, block), BF16)
    out = pl.pallas_call(
        functools.partial(kernel, peers, lines),
        out_shape=jax.ShapeDtypeStruct((faces, samples, block), BF16),
        in_specs=[hbm] * 11,
        out_specs=vmem,
        scratch_shapes=[
            pltpu.SMEM((faces,), jnp.int32),
            pltpu.SMEM((faces,), F32),
            stack,
            pltpu.VMEM((faces, block), jnp.int32),
            pltpu.VMEM((1, vertex_unknowns.shape[-1]), jnp.int32),
            pltpu.VMEM((channels, channels), F32),
            pltpu.VMEM((interface, interface), BF16),
            pltpu.VMEM((interface, primal), BF16),
            pltpu.VMEM((lines * primal, primal), BF16),
            pltpu.VMEM((lines * primal, channels), BF16),
            pltpu.VMEM((channels, primal), BF16),
            stack,
            stack,
            pltpu.VMEM((faces, 8, block), jnp.int32),
            pltpu.VMEM((faces, 8, block), jnp.int32),
            pltpu.VMEM((faces, block, block), BF16),
            stack,
            pltpu.VMEM((samples, interface), BF16),
            pltpu.VMEM((faces, samples, block), F32),
            pltpu.VMEM((faces, 8, block), F32),
            pltpu.VMEM((lines, samples, primal), BF16),
            pltpu.VMEM((2, peers // 2, channels, channels), BF16),
            pltpu.VMEM((peers // 4, 3 * channels, 3 * channels), BF16),
            pltpu.VMEM((peers // 4, channels, 4 * channels), BF16),
            pltpu.VMEM((samples, channels), F32),
            pltpu.VMEM((share * peers, rows, channels), F32),
            pltpu.VMEM((peers, rows, channels), F32),
            pltpu.VMEM((samples, channels), F32),
            stack,
            stack,
            stack,
            dma((11,)),
            dma((4,)),
            dma((4,)),
            dma((4,)),
            dma((4,)),
            dma((lines,)),
            dma((lines,)),
            dma((peers // 2,)),
            dma((peers // 2,)),
            dma,
            dma,
            dma((share * peers,)),
            dma((share * peers,)),
            dma((share * peers,)),
            dma((share * peers,)),
            dma((4,)),
            dma((4,)),
        ],
        compiler_params=pltpu.CompilerParams(
            collective_id=0, has_side_effects=True, vmem_limit_bytes=60 * 1024 * 1024
        ),
    )(
        face_slot[0, 0],
        face_scale[0, 0],
        residual_parts[0, 0],
        face_order[0, 0],
        vertex_unknowns[0],
        chain_transfer[0],
        front_inverse[0, 0],
        coarse_basis[0, 0],
        coarse_inverse[0],
        thermal_handoff[0],
        coupling_in[0],
    )
    return out[None, None]


def solution(mesh):
    placed = (
        P("sub", "coarse", None, None, None),
        P("sub", "coarse", None),
        P("sub", "coarse", None, None),
        P("sub", "coarse", None),
        P("sub", "coarse", None),
        P("sub", "coarse", None, None),
        P("sub", "coarse", None, None),
        P("sub", None, "coarse"),
        P("sub", None, None),
        P("sub", None, None),
        P("sub", None, "coarse"),
    )
    return jax.shard_map(
        functools.partial(per_device, mesh.shape["sub"], mesh.shape["coarse"]),
        mesh=mesh,
        in_specs=placed,
        out_specs=P("sub", "coarse", None, None, None),
        check_vma=False,
    )
```

```python
import functools

import jax
import jax.numpy as jnp
from jax import lax
from jax.experimental import pallas as pl
from jax.experimental.pallas import tpu as pltpu
from jax.sharding import PartitionSpec as P

MESH = pl.DeviceIdType.MESH
F32, BF16 = jnp.float32, jnp.bfloat16
NT = (((1,), (1,)), ((), ()))


def dot(a, b):
    return jnp.dot(a, b, preferred_element_type=F32)


def dot_nt(a, b):
    return lax.dot_general(a, b, NT, preferred_element_type=F32)


def split_rows(x):
    high = x.astype(BF16).astype(F32)
    return jnp.concatenate([high, x - high], axis=0).astype(BF16)


def shares(samples, peers, lines):
    rows = samples // peers
    return lines if rows % (8 * lines) == 0 else 1


def kernel(
    peers,
    lines,
    slot_hbm,
    scale_hbm,
    parts_hbm,
    order_hbm,
    primal_hbm,
    transfer_hbm,
    inverse_hbm,
    basis_hbm,
    line_hbm,
    handoff_hbm,
    coupling_hbm,
    out_ref,
    slot_ref,
    scale_ref,
    parts_ref,
    order_ref,
    primal_ref,
    transfer_ref,
    inverse,
    basis,
    line,
    handoff,
    coupling,
    face_out,
    face_in,
    order_out,
    order_in,
    table,
    placed,
    residual,
    dual,
    mask,
    coarse,
    transfers,
    within,
    through,
    inflow,
    heat_in,
    heat_out,
    carried,
    weighted,
    face_out2,
    face_in2,
    load_sem,
    face_send,
    face_recv,
    order_send,
    order_recv,
    coarse_send,
    coarse_recv,
    chip_send,
    chip_recv,
    core_send,
    core_recv,
    heat_send,
    heat_recv,
    back_send,
    back_recv,
    face_send2,
    face_recv2,
):
    me, col = lax.axis_index("sub"), lax.axis_index("coarse")
    faces, samples, block = parts_ref.shape
    primal = basis.shape[1]
    share = shares(samples, peers, lines)
    rows = samples // (peers * share)
    chips = peers // 2
    chip, core = me // 2, lax.rem(me, 2)

    loads = [
        pltpu.make_async_copy(source, target, load_sem.at[i])
        for i, (source, target) in enumerate(
            [
                (slot_hbm, slot_ref),
                (scale_hbm, scale_ref),
                (parts_hbm, parts_ref),
                (order_hbm, order_ref),
                (transfer_hbm, transfer_ref),
                (primal_hbm, primal_ref),
                (basis_hbm, basis),
                (handoff_hbm, handoff),
                (inverse_hbm, inverse),
                (line_hbm, line),
                (coupling_hbm, coupling),
            ]
        )
    ]
    for load in loads:
        load.start()

    barrier = pltpu.get_barrier_semaphore()

    def other(n):
        return lax.rem(me + lax.rem(n, peers), peers), lax.rem(col + n // peers, lines)

    @pl.loop(1, peers * share)
    def _(n):
        pl.semaphore_signal(barrier, inc=1, device_id=other(n), device_id_type=MESH)

    if share == 1:

        @pl.loop(1, lines)
        def _(k):
            pl.semaphore_signal(
                barrier, inc=1, device_id=(me, lax.rem(col + k, lines)), device_id_type=MESH
            )

    for load in loads[:5]:
        load.wait()
    slots = [slot_ref[d] for d in range(4)]
    direction = []
    for s in range(4):
        found = jnp.int32(0)
        for d in range(1, 4):
            found = jnp.where(slots[d] == s, d, found)
        direction.append(found)
    scales = [scale_ref[direction[s]] for s in range(4)]

    for d in range(4):
        face_out[d] = parts_ref[slots[d]]
        own = order_ref[pl.ds(slots[d], 1), :]
        order_out[d] = jnp.broadcast_to(own, (8, block))
    transfers[core, chip] = transfer_ref[...].astype(BF16)

    pl.semaphore_wait(barrier, peers * share - 1 + (lines - 1 if share == 1 else 0))

    exists = [me > 0, me < peers - 1, col > 0, col < lines - 1]
    beside = [
        (jnp.maximum(me - 1, 0), col),
        (jnp.minimum(me + 1, peers - 1), col),
        (me, jnp.maximum(col - 1, 0)),
        (me, jnp.minimum(col + 1, lines - 1)),
    ]

    def face_copy(source, target, send, recv, d, at):
        return pltpu.make_async_remote_copy(
            src_ref=source.at[d],
            dst_ref=target.at[at],
            send_sem=send.at[d],
            recv_sem=recv.at[at],
            device_id=beside[d],
            device_id_type=MESH,
        )

    def orders(d, at):
        return face_copy(order_out, order_in, order_send, order_recv, d, at)

    def first(d, at):
        return face_copy(face_out, face_in, face_send, face_recv, d, at)

    def second(d, at):
        return face_copy(face_out2, face_in2, face_send2, face_recv2, d, at)

    for d in (2, 3, 0, 1):

        @pl.when(exists[d])
        def _():
            orders(d, d ^ 1).start()
            first(d, d ^ 1).start()

    def to_chip(target, source):
        return pltpu.make_async_remote_copy(
            src_ref=transfers.at[core, source],
            dst_ref=transfers.at[core, source],
            send_sem=chip_send,
            recv_sem=chip_recv,
            device_id=(target * 2 + core, col),
            device_id_type=MESH,
        )

    @pl.loop(1, chips)
    def _(k):
        to_chip(lax.rem(chip + k, chips), chip).start()

    loads[5].wait()
    ids = primal_ref[...]
    count = ids.shape[1]
    groups = faces * block // 128
    group_hit = jnp.where(lax.broadcasted_iota(jnp.int32, (groups, count), 0) == ids // 128, 1.0, 0.0)
    lane_hit = jnp.where(lax.broadcasted_iota(jnp.int32, (128, count), 0) == ids % 128, 1.0, 0.0)
    kept = 1.0 - dot_nt(group_hit.astype(BF16), lane_hit.astype(BF16))
    per_face = block // 128
    for s in range(4):
        row = jnp.concatenate(
            [kept[s * per_face + t : s * per_face + t + 1] for t in range(per_face)], axis=1
        )
        mask[s] = jnp.broadcast_to(row, (8, block))

    for d in (0, 1, 2, 3):

        @pl.when(exists[d])
        def _():
            position = lax.broadcasted_iota(jnp.int32, (block, block), 0)
            own_table = jnp.where(position == order_out[d, 0:1, :], 1.0, 0.0).astype(BF16)
            orders(d, d).wait_recv()
            theirs = order_in[d]
            halves = jnp.concatenate([theirs // 16, theirs % 16], axis=0)
            found = dot_nt(halves.astype(F32).astype(BF16), own_table)
            joined = (found[0:1] * 16.0 + found[8:9]).astype(jnp.int32)
            table[d] = jnp.where(position == joined, 1.0, 0.0).astype(BF16)

    def place(d, copy, landed):
        @pl.when(exists[d])
        def _():
            copy(d, d).wait_recv()
            placed[d] = dot(landed[d], table[d]).astype(BF16)

        @pl.when(jnp.logical_not(exists[d]))
        def _():
            placed[d] = jnp.zeros((samples, block), BF16)

    for d in (0, 1, 2, 3):
        place(d, first, face_in)
    for s in range(4):
        total = parts_ref[s].astype(F32) + placed[direction[s]].astype(F32)
        residual[:, s * block : (s + 1) * block] = (scales[s] * total).astype(BF16)

    loads[6].wait()
    own_coarse = dot(residual[...], basis[...])
    coarse[col] = own_coarse.astype(BF16)

    def to_line(target, source):
        return pltpu.make_async_remote_copy(
            src_ref=coarse.at[source],
            dst_ref=coarse.at[source],
            send_sem=coarse_send.at[target],
            recv_sem=coarse_recv.at[source],
            device_id=(me, target),
            device_id_type=MESH,
        )

    def line_start():
        @pl.loop(1, lines)
        def _(k):
            to_line(lax.rem(col + k, lines), col).start()

    def line_wait():
        @pl.loop(1, lines)
        def _(k):
            to_line(col, lax.rem(col + k, lines)).wait_recv()

    def place_of(p, c):
        return (c if share > 1 else 0) * peers + p

    def chunk(p, c):
        first_row = (p * share + (c if share > 1 else 0)) * rows
        return pl.ds(pl.multiple_of(first_row, rows), rows)

    def to_samples(target, source):
        return pltpu.make_async_remote_copy(
            src_ref=inflow.at[chunk(*target)],
            dst_ref=heat_in.at[place_of(*source)],
            send_sem=heat_send,
            recv_sem=heat_recv,
            device_id=target,
            device_id_type=MESH,
        )

    def to_lines(target, source):
        return pltpu.make_async_remote_copy(
            src_ref=heat_out.at[target[0]],
            dst_ref=carried.at[chunk(*source)],
            send_sem=back_send,
            recv_sem=back_recv,
            device_id=target,
            device_id_type=MESH,
        )

    def await_bytes(part, sem):
        pltpu.make_async_copy(part, part, sem).wait()

    def await_chips(sem):
        await_bytes(transfers.at[0, pl.ds(0, chips - 1)], sem)

    def await_heat(sem):
        await_bytes(heat_in.at[pl.ds(0, peers * share - 1)], sem)

    def await_back(sem):
        await_bytes(carried.at[pl.ds(0, (peers * share - 1) * rows)], sem)

    here = (me, col)
    loads[7].wait()
    if share > 1:
        own_rows = pl.ds(pl.multiple_of(col * primal, primal), primal)
        inflow[...] = dot(coarse[col], handoff[own_rows, :])
    else:
        line_start()
        line_wait()
        heat = jnp.zeros((samples, handoff.shape[1]), F32)
        for q in range(lines):
            heat += dot(coarse[q], handoff[q * primal : (q + 1) * primal, :])
        inflow[...] = heat

    @pl.loop(1, peers * share)
    def _(n):
        to_samples(other(n), here).start()

    if share > 1:
        line_start()
    heat_in[place_of(*here)] = inflow[chunk(*here), :]

    await_chips(chip_recv)

    def to_core(which):
        return pltpu.make_async_remote_copy(
            src_ref=transfers.at[which],
            dst_ref=transfers.at[which],
            send_sem=core_send,
            recv_sem=core_recv,
            device_id=(chip * 2 + 1 - core, col),
            device_id_type=MESH,
        )

    to_core(core).start()

    for s in range(4):
        at = slice(s * block, (s + 1) * block)
        residual[:, at] = (residual[:, at].astype(F32) * mask[s, 0:1, :]).astype(BF16)
    loads[8].wait()

    def dual_face(s):
        at = pl.ds(pl.multiple_of(s * block, block), block)
        dual[s] = dot(residual[...], inverse[:, at]) * mask[s, 0:1, :]

    pl.loop(0, 2)(dual_face)

    to_core(1 - core).wait_recv()
    width = handoff.shape[1]
    groups4 = peers // 4
    nothing = jnp.zeros((width, width), BF16)
    for g in range(groups4):
        t0, t1 = transfers[0, 2 * g], transfers[1, 2 * g]
        t2, t3 = transfers[0, 2 * g + 1], transfers[1, 2 * g + 1]
        t01 = dot(t0, t1).astype(BF16)
        t12 = dot(t1, t2).astype(BF16)
        t23 = dot(t2, t3).astype(BF16)
        t012 = dot(t01, t2).astype(BF16)
        t123 = dot(t12, t3).astype(BF16)
        t0123 = dot(t012, t3).astype(BF16)
        for k, tile in enumerate((t0, t01, t012, t0123)):
            through[g, :, k * width : (k + 1) * width] = tile
        table3 = ((t1, t12, t123), (nothing, t2, t23), (nothing, nothing, t3))
        for i in range(3):
            for k in range(3):
                within[g, i * width : (i + 1) * width, k * width : (k + 1) * width] = table3[i][k]

    await_heat(heat_recv)

    local = []
    for g in range(groups4):
        own = []
        for i in range(4):
            total = heat_in[4 * g + i]
            for c in range(1, share):
                total = total + heat_in[c * peers + 4 * g + i]
            own.append(total)
        split = dot(split_rows(jnp.concatenate(own[:3], axis=1)), within[g])
        split = split[:rows] + split[rows:]
        local.append(
            [own[0]] + [split[:, k * width : (k + 1) * width] + own[k + 1] for k in range(3)]
        )
    state = jnp.zeros((rows, width), F32)
    for g in range(groups4):
        heat_out[4 * g] = state
        split = dot(split_rows(state), through[g])
        split = split[:rows] + split[rows:]
        ahead = [split[:, k * width : (k + 1) * width] + local[g][k] for k in range(4)]
        for k in range(3):
            heat_out[4 * g + k + 1] = ahead[k]
        state = ahead[3]

        @pl.loop(0, 4 * share)
        def _(n):
            p, c = 4 * g + lax.rem(n, 4), n // 4

            @pl.when(jnp.logical_or(p != me, c != 0))
            def _():
                to_lines((p, lax.rem(col + c, lines)), here).start()

    carried[chunk(*here), :] = heat_out[me]

    pl.loop(2, 4)(dual_face)

    if share > 1:
        line_wait()
    loads[9].wait()
    base = jnp.zeros((samples, primal), F32)
    for q in range(lines):
        base += dot(coarse[q], line[q * primal : (q + 1) * primal, :])
    loads[10].wait()

    await_back(back_recv)

    coupled = dot(split_rows(carried[...]), coupling[...])
    answer = (base + coupled[:samples] + coupled[samples:]).astype(BF16)
    for s in range(4):
        found = dual[s] + dot_nt(answer, basis[s * block : (s + 1) * block, :])
        weighted[s] = (scales[s] * found).astype(BF16)
    for d in (2, 3, 0, 1):
        face_out2[d] = weighted[slots[d]]

        @pl.when(exists[d])
        def _():
            second(d, d ^ 1).start()

    for d in (0, 1, 2, 3):
        place(d, second, face_in2)
    for s in range(4):
        total = weighted[s].astype(F32) + placed[direction[s]].astype(F32)
        out_ref[s] = total.astype(BF16)

    for d in range(4):

        @pl.when(exists[d])
        def _():
            orders(d, d ^ 1).wait_send()
            first(d, d ^ 1).wait_send()
            second(d, d ^ 1).wait_send()

    await_chips(chip_send)

    to_core(core).wait_send()

    @pl.loop(1, lines)
    def _(k):
        to_line(lax.rem(col + k, lines), col).wait_send()

    await_heat(heat_send)
    await_back(back_send)


def per_device(
    peers,
    lines,
    residual_parts,
    face_slot,
    face_order,
    face_scale,
    vertex_unknowns,
    front_inverse,
    coarse_basis,
    coarse_inverse,
    thermal_handoff,
    chain_transfer,
    coupling_in,
):
    faces, samples, block = residual_parts.shape[2:]
    interface = faces * block
    primal = coarse_basis.shape[-1]
    channels = chain_transfer.shape[-1]
    share = shares(samples, peers, lines)
    rows = samples // (peers * share)
    dma = pltpu.SemaphoreType.DMA
    vmem, hbm = (pl.BlockSpec(memory_space=space) for space in (pltpu.VMEM, pltpu.HBM))
    stack = pltpu.VMEM((faces, samples, block), BF16)
    out = pl.pallas_call(
        functools.partial(kernel, peers, lines),
        out_shape=pltpu.VMEM((faces, samples, block), BF16),
        in_specs=[hbm] * 11,
        out_specs=vmem,
        scratch_shapes=[
            pltpu.SMEM((faces,), jnp.int32),
            pltpu.SMEM((faces,), F32),
            stack,
            pltpu.VMEM((faces, block), jnp.int32),
            pltpu.VMEM((1, vertex_unknowns.shape[-1]), jnp.int32),
            pltpu.VMEM((channels, channels), F32),
            pltpu.VMEM((interface, interface), BF16),
            pltpu.VMEM((interface, primal), BF16),
            pltpu.VMEM((lines * primal, primal), BF16),
            pltpu.VMEM((lines * primal, channels), BF16),
            pltpu.VMEM((channels, primal), BF16),
            stack,
            stack,
            pltpu.VMEM((faces, 8, block), jnp.int32),
            pltpu.VMEM((faces, 8, block), jnp.int32),
            pltpu.VMEM((faces, block, block), BF16),
            stack,
            pltpu.VMEM((samples, interface), BF16),
            pltpu.VMEM((faces, samples, block), F32),
            pltpu.VMEM((faces, 8, block), F32),
            pltpu.VMEM((lines, samples, primal), BF16),
            pltpu.VMEM((2, peers // 2, channels, channels), BF16),
            pltpu.VMEM((peers // 4, 3 * channels, 3 * channels), BF16),
            pltpu.VMEM((peers // 4, channels, 4 * channels), BF16),
            pltpu.VMEM((samples, channels), F32),
            pltpu.VMEM((share * peers, rows, channels), F32),
            pltpu.VMEM((peers, rows, channels), F32),
            pltpu.VMEM((samples, channels), F32),
            stack,
            stack,
            stack,
            dma((11,)),
            dma((4,)),
            dma((4,)),
            dma((4,)),
            dma((4,)),
            dma((lines,)),
            dma((lines,)),
            dma,
            dma,
            dma,
            dma,
            dma,
            dma,
            dma,
            dma,
            dma((4,)),
            dma((4,)),
        ],
        compiler_params=pltpu.CompilerParams(
            collective_id=0, has_side_effects=True, vmem_limit_bytes=60 * 1024 * 1024
        ),
    )(
        face_slot[0, 0],
        face_scale[0, 0],
        residual_parts[0, 0],
        face_order[0, 0],
        vertex_unknowns[0],
        chain_transfer[0],
        front_inverse[0, 0],
        coarse_basis[0, 0],
        coarse_inverse[0],
        thermal_handoff[0],
        coupling_in[0],
    )
    return out[None, None]


def solution(mesh):
    placed = (
        P("sub", "coarse", None, None, None),
        P("sub", "coarse", None),
        P("sub", "coarse", None, None),
        P("sub", "coarse", None),
        P("sub", "coarse", None),
        P("sub", "coarse", None, None),
        P("sub", "coarse", None, None),
        P("sub", None, "coarse"),
        P("sub", None, None),
        P("sub", None, None),
        P("sub", None, "coarse"),
    )
    return jax.shard_map(
        functools.partial(per_device, mesh.shape["sub"], mesh.shape["coarse"]),
        mesh=mesh,
        in_specs=placed,
        out_specs=P("sub", "coarse", None, None, None),
        check_vma=False,
    )
```

```python
import functools

import jax
import jax.numpy as jnp
from jax import lax
from jax.experimental import pallas as pl
from jax.experimental.pallas import tpu as pltpu
from jax.sharding import PartitionSpec as P

MESH = pl.DeviceIdType.MESH
F32, BF16 = jnp.float32, jnp.bfloat16
NT = (((1,), (1,)), ((), ()))


def dot(a, b):
    return jnp.dot(a, b, preferred_element_type=F32)


def dot_nt(a, b):
    return lax.dot_general(a, b, NT, preferred_element_type=F32)


def split_rows(x):
    high = x.astype(BF16).astype(F32)
    return jnp.concatenate([high, x - high], axis=0).astype(BF16)


def shares(samples, peers, lines):
    rows = samples // peers
    return lines if rows % (8 * lines) == 0 else 1


def kernel(
    peers,
    lines,
    slot_hbm,
    scale_hbm,
    parts_hbm,
    order_hbm,
    primal_hbm,
    transfer_hbm,
    inverse_hbm,
    basis_hbm,
    line_hbm,
    handoff_hbm,
    coupling_hbm,
    out_ref,
    slot_ref,
    scale_ref,
    parts_ref,
    order_ref,
    primal_ref,
    transfer_ref,
    inverse,
    basis,
    line,
    handoff,
    coupling,
    face_out,
    face_in,
    order_out,
    order_in,
    table,
    placed,
    residual,
    dual,
    mask,
    coarse,
    transfers,
    within,
    through,
    inflow,
    heat_in,
    heat_out,
    carried,
    weighted,
    face_out2,
    face_in2,
    basis_out,
    basis_in,
    answer_out,
    answer_in,
    load_sem,
    face_send,
    face_recv,
    order_send,
    order_recv,
    coarse_send,
    coarse_recv,
    chip_send,
    chip_recv,
    core_send,
    core_recv,
    heat_send,
    heat_recv,
    back_send,
    back_recv,
    face_send2,
    face_recv2,
    basis_send,
    basis_recv,
    answer_send,
    answer_recv,
):
    me, col = lax.axis_index("sub"), lax.axis_index("coarse")
    faces, samples, block = parts_ref.shape
    primal = basis.shape[2]
    share = shares(samples, peers, lines)
    rows = samples // (peers * share)
    chips = peers // 2
    chip, core = me // 2, lax.rem(me, 2)

    loads = [
        pltpu.make_async_copy(source, target, load_sem.at[i])
        for i, (source, target) in enumerate(
            [
                (slot_hbm, slot_ref),
                (scale_hbm, scale_ref),
                (parts_hbm, parts_ref),
                (order_hbm, order_ref),
                (transfer_hbm, transfer_ref),
                (primal_hbm, primal_ref),
                (basis_hbm, basis),
                (handoff_hbm, handoff),
                (inverse_hbm, inverse),
                (line_hbm, line),
                (coupling_hbm, coupling),
            ]
        )
    ]
    for load in loads:
        load.start()

    barrier = pltpu.get_barrier_semaphore()

    def other(n):
        return lax.rem(me + lax.rem(n, peers), peers), lax.rem(col + n // peers, lines)

    @pl.loop(1, peers * share)
    def _(n):
        pl.semaphore_signal(barrier, inc=1, device_id=other(n), device_id_type=MESH)

    if share == 1:

        @pl.loop(1, lines)
        def _(k):
            pl.semaphore_signal(
                barrier, inc=1, device_id=(me, lax.rem(col + k, lines)), device_id_type=MESH
            )

    for load in loads[:5]:
        load.wait()
    slots = [slot_ref[d] for d in range(4)]
    direction = []
    for s in range(4):
        found = jnp.int32(0)
        for d in range(1, 4):
            found = jnp.where(slots[d] == s, d, found)
        direction.append(found)
    scales = [scale_ref[direction[s]] for s in range(4)]

    for d in range(4):
        face_out[d] = parts_ref[slots[d]]
        own = order_ref[pl.ds(slots[d], 1), :]
        order_out[d] = jnp.broadcast_to(own, (8, block))
    transfers[core, chip] = transfer_ref[...].astype(BF16)

    pl.semaphore_wait(barrier, peers * share - 1 + (lines - 1 if share == 1 else 0))

    exists = [me > 0, me < peers - 1, col > 0, col < lines - 1]
    beside = [
        (jnp.maximum(me - 1, 0), col),
        (jnp.minimum(me + 1, peers - 1), col),
        (me, jnp.maximum(col - 1, 0)),
        (me, jnp.minimum(col + 1, lines - 1)),
    ]

    def face_copy(source, target, send, recv, d, at):
        return pltpu.make_async_remote_copy(
            src_ref=source.at[d],
            dst_ref=target.at[at],
            send_sem=send.at[d],
            recv_sem=recv.at[at],
            device_id=beside[d],
            device_id_type=MESH,
        )

    def orders(d, at):
        return face_copy(order_out, order_in, order_send, order_recv, d, at)

    def first(d, at):
        return face_copy(face_out, face_in, face_send, face_recv, d, at)

    def second(d, at):
        return face_copy(face_out2, face_in2, face_send2, face_recv2, d, at)

    def bases(d, at):
        return face_copy(basis_out, basis_in, basis_send, basis_recv, d, at)

    def answers(d, at):
        return pltpu.make_async_remote_copy(
            src_ref=answer_out,
            dst_ref=answer_in.at[at],
            send_sem=answer_send.at[d],
            recv_sem=answer_recv.at[at],
            device_id=beside[d],
            device_id_type=MESH,
        )

    for d in (2, 3, 0, 1):

        @pl.when(exists[d])
        def _():
            orders(d, d ^ 1).start()
            first(d, d ^ 1).start()

    def to_chip(target, source):
        return pltpu.make_async_remote_copy(
            src_ref=transfers.at[core, source],
            dst_ref=transfers.at[core, source],
            send_sem=chip_send,
            recv_sem=chip_recv,
            device_id=(target * 2 + core, col),
            device_id_type=MESH,
        )

    @pl.loop(1, chips)
    def _(k):
        to_chip(lax.rem(chip + k, chips), chip).start()

    loads[5].wait()
    ids = primal_ref[...]
    count = ids.shape[1]
    groups = faces * block // 128
    group_hit = jnp.where(lax.broadcasted_iota(jnp.int32, (groups, count), 0) == ids // 128, 1.0, 0.0)
    lane_hit = jnp.where(lax.broadcasted_iota(jnp.int32, (128, count), 0) == ids % 128, 1.0, 0.0)
    kept = 1.0 - dot_nt(group_hit.astype(BF16), lane_hit.astype(BF16))
    per_face = block // 128
    for s in range(4):
        row = jnp.concatenate(
            [kept[s * per_face + t : s * per_face + t + 1] for t in range(per_face)], axis=1
        )
        mask[s] = jnp.broadcast_to(row, (8, block))

    for d in (0, 1, 2, 3):

        @pl.when(exists[d])
        def _():
            position = lax.broadcasted_iota(jnp.int32, (block, block), 0)
            own_table = jnp.where(position == order_out[d, 0:1, :], 1.0, 0.0).astype(BF16)
            orders(d, d).wait_recv()
            theirs = order_in[d]
            halves = jnp.concatenate([theirs // 16, theirs % 16], axis=0)
            found = dot_nt(halves.astype(F32).astype(BF16), own_table)
            joined = (found[0:1] * 16.0 + found[8:9]).astype(jnp.int32)
            table[d] = jnp.where(position == joined, 1.0, 0.0).astype(BF16)

    def place(d, copy, landed):
        @pl.when(exists[d])
        def _():
            copy(d, d).wait_recv()
            placed[d] = dot(landed[d], table[d]).astype(BF16)

        @pl.when(jnp.logical_not(exists[d]))
        def _():
            placed[d] = jnp.zeros((samples, block), BF16)

    for d in (0, 1, 2, 3):
        place(d, first, face_in)
    for s in range(4):
        total = parts_ref[s].astype(F32) + placed[direction[s]].astype(F32)
        residual[:, s * block : (s + 1) * block] = (scales[s] * total).astype(BF16)

    loads[6].wait()
    own_coarse = dot(residual[...], basis[...].reshape(faces * block, primal))
    coarse[col] = own_coarse.astype(BF16)

    def to_line(target, source):
        return pltpu.make_async_remote_copy(
            src_ref=coarse.at[source],
            dst_ref=coarse.at[source],
            send_sem=coarse_send.at[target],
            recv_sem=coarse_recv.at[source],
            device_id=(me, target),
            device_id_type=MESH,
        )

    def line_start():
        @pl.loop(1, lines)
        def _(k):
            to_line(lax.rem(col + k, lines), col).start()

    def line_wait():
        @pl.loop(1, lines)
        def _(k):
            to_line(col, lax.rem(col + k, lines)).wait_recv()

    def place_of(p, c):
        return (c if share > 1 else 0) * peers + p

    def chunk(p, c):
        first_row = (p * share + (c if share > 1 else 0)) * rows
        return pl.ds(pl.multiple_of(first_row, rows), rows)

    def to_samples(target, source):
        return pltpu.make_async_remote_copy(
            src_ref=inflow.at[chunk(*target)],
            dst_ref=heat_in.at[place_of(*source)],
            send_sem=heat_send,
            recv_sem=heat_recv,
            device_id=target,
            device_id_type=MESH,
        )

    def to_lines(target, source):
        return pltpu.make_async_remote_copy(
            src_ref=heat_out.at[target[0]],
            dst_ref=carried.at[chunk(*source)],
            send_sem=back_send,
            recv_sem=back_recv,
            device_id=target,
            device_id_type=MESH,
        )

    def await_bytes(part, sem):
        pltpu.make_async_copy(part, part, sem).wait()

    def await_chips(sem):
        await_bytes(transfers.at[0, pl.ds(0, chips - 1)], sem)

    def await_heat(sem):
        await_bytes(heat_in.at[pl.ds(0, peers * share - 1)], sem)

    def await_back(sem):
        await_bytes(carried.at[pl.ds(0, (peers * share - 1) * rows)], sem)

    here = (me, col)
    loads[7].wait()
    if share > 1:
        own_rows = pl.ds(pl.multiple_of(col * primal, primal), primal)
        inflow[...] = dot(coarse[col], handoff[own_rows, :])
    else:
        line_start()
        line_wait()
        heat = jnp.zeros((samples, handoff.shape[1]), F32)
        for q in range(lines):
            heat += dot(coarse[q], handoff[q * primal : (q + 1) * primal, :])
        inflow[...] = heat

    @pl.loop(1, peers * share)
    def _(n):
        to_samples(other(n), here).start()

    if share > 1:
        line_start()
    for d in range(4):
        basis_out[d] = basis[slots[d]]

        @pl.when(exists[d])
        def _():
            bases(d, d ^ 1).start()

    heat_in[place_of(*here)] = inflow[chunk(*here), :]

    await_chips(chip_recv)

    def to_core(which):
        return pltpu.make_async_remote_copy(
            src_ref=transfers.at[which],
            dst_ref=transfers.at[which],
            send_sem=core_send,
            recv_sem=core_recv,
            device_id=(chip * 2 + 1 - core, col),
            device_id_type=MESH,
        )

    to_core(core).start()

    for s in range(4):
        at = slice(s * block, (s + 1) * block)
        residual[:, at] = (residual[:, at].astype(F32) * mask[s, 0:1, :]).astype(BF16)
    loads[8].wait()

    def dual_face(s):
        at = pl.ds(pl.multiple_of(s * block, block), block)
        dual[s] = dot(residual[...], inverse[:, at]) * mask[s, 0:1, :]

    pl.loop(0, 4)(dual_face)
    for d in (2, 3, 0, 1):
        face_out2[d] = dual[slots[d]].astype(BF16)

        @pl.when(exists[d])
        def _():
            second(d, d ^ 1).start()

    to_core(1 - core).wait_recv()
    width = handoff.shape[1]
    groups4 = peers // 4
    nothing = jnp.zeros((width, width), BF16)
    for g in range(groups4):
        t0, t1 = transfers[0, 2 * g], transfers[1, 2 * g]
        t2, t3 = transfers[0, 2 * g + 1], transfers[1, 2 * g + 1]
        t01 = dot(t0, t1).astype(BF16)
        t12 = dot(t1, t2).astype(BF16)
        t23 = dot(t2, t3).astype(BF16)
        t012 = dot(t01, t2).astype(BF16)
        t123 = dot(t12, t3).astype(BF16)
        t0123 = dot(t012, t3).astype(BF16)
        for k, tile in enumerate((t0, t01, t012, t0123)):
            through[g, :, k * width : (k + 1) * width] = tile
        table3 = ((t1, t12, t123), (nothing, t2, t23), (nothing, nothing, t3))
        for i in range(3):
            for k in range(3):
                within[g, i * width : (i + 1) * width, k * width : (k + 1) * width] = table3[i][k]

    await_heat(heat_recv)

    local = []
    for g in range(groups4):
        own = []
        for i in range(4):
            total = heat_in[4 * g + i]
            for c in range(1, share):
                total = total + heat_in[c * peers + 4 * g + i]
            own.append(total)
        split = dot(split_rows(jnp.concatenate(own[:3], axis=1)), within[g])
        split = split[:rows] + split[rows:]
        local.append(
            [own[0]] + [split[:, k * width : (k + 1) * width] + own[k + 1] for k in range(3)]
        )
    state = jnp.zeros((rows, width), F32)
    for g in range(groups4):
        heat_out[4 * g] = state
        split = dot(split_rows(state), through[g])
        split = split[:rows] + split[rows:]
        ahead = [split[:, k * width : (k + 1) * width] + local[g][k] for k in range(4)]
        for k in range(3):
            heat_out[4 * g + k + 1] = ahead[k]
        state = ahead[3]

        @pl.loop(0, 4 * share)
        def _(n):
            p, c = 4 * g + lax.rem(n, 4), n // 4

            @pl.when(jnp.logical_or(p != me, c != 0))
            def _():
                to_lines((p, lax.rem(col + c, lines)), here).start()

    carried[chunk(*here), :] = heat_out[me]

    if share > 1:
        line_wait()
    loads[9].wait()
    base = jnp.zeros((samples, primal), F32)
    for q in range(lines):
        base += dot(coarse[q], line[q * primal : (q + 1) * primal, :])
    loads[10].wait()

    await_back(back_recv)

    coupled = dot(split_rows(carried[...]), coupling[...])
    answer = (base + coupled[:samples] + coupled[samples:]).astype(BF16)
    answer_out[...] = answer
    for d in (2, 3, 0, 1):

        @pl.when(exists[d])
        def _():
            answers(d, d ^ 1).start()

    for s in range(4):
        found = dual[s] + dot_nt(answer, basis[s])
        weighted[s] = (scales[s] * found).astype(BF16)

    for d in (0, 1, 2, 3):

        @pl.when(exists[d])
        def _():
            bases(d, d).wait_recv()
            second(d, d).wait_recv()
            answers(d, d).wait_recv()
            theirs = face_in2[d].astype(F32) + dot_nt(answer_in[d], basis_in[d])
            theirs = ((1.0 - scale_ref[d]) * theirs).astype(BF16)
            placed[d] = dot(theirs, table[d]).astype(BF16)

    for s in range(4):
        total = weighted[s].astype(F32) + placed[direction[s]].astype(F32)
        out_ref[s] = total.astype(BF16)

    for d in range(4):

        @pl.when(exists[d])
        def _():
            orders(d, d ^ 1).wait_send()
            first(d, d ^ 1).wait_send()
            second(d, d ^ 1).wait_send()
            bases(d, d ^ 1).wait_send()
            answers(d, d ^ 1).wait_send()

    await_chips(chip_send)

    to_core(core).wait_send()

    @pl.loop(1, lines)
    def _(k):
        to_line(lax.rem(col + k, lines), col).wait_send()

    await_heat(heat_send)
    await_back(back_send)


def per_device(
    peers,
    lines,
    residual_parts,
    face_slot,
    face_order,
    face_scale,
    vertex_unknowns,
    front_inverse,
    coarse_basis,
    coarse_inverse,
    thermal_handoff,
    chain_transfer,
    coupling_in,
):
    faces, samples, block = residual_parts.shape[2:]
    interface = faces * block
    primal = coarse_basis.shape[-1]
    channels = chain_transfer.shape[-1]
    share = shares(samples, peers, lines)
    rows = samples // (peers * share)
    dma = pltpu.SemaphoreType.DMA
    vmem, hbm = (pl.BlockSpec(memory_space=space) for space in (pltpu.VMEM, pltpu.HBM))
    stack = pltpu.VMEM((faces, samples, block), BF16)
    out = pl.pallas_call(
        functools.partial(kernel, peers, lines),
        out_shape=pltpu.VMEM((faces, samples, block), BF16),
        in_specs=[hbm] * 11,
        out_specs=vmem,
        scratch_shapes=[
            pltpu.SMEM((faces,), jnp.int32),
            pltpu.SMEM((faces,), F32),
            stack,
            pltpu.VMEM((faces, block), jnp.int32),
            pltpu.VMEM((1, vertex_unknowns.shape[-1]), jnp.int32),
            pltpu.VMEM((channels, channels), F32),
            pltpu.VMEM((interface, interface), BF16),
            pltpu.VMEM((faces, block, primal), BF16),
            pltpu.VMEM((lines * primal, primal), BF16),
            pltpu.VMEM((lines * primal, channels), BF16),
            pltpu.VMEM((channels, primal), BF16),
            stack,
            stack,
            pltpu.VMEM((faces, 8, block), jnp.int32),
            pltpu.VMEM((faces, 8, block), jnp.int32),
            pltpu.VMEM((faces, block, block), BF16),
            stack,
            pltpu.VMEM((samples, interface), BF16),
            pltpu.VMEM((faces, samples, block), F32),
            pltpu.VMEM((faces, 8, block), F32),
            pltpu.VMEM((lines, samples, primal), BF16),
            pltpu.VMEM((2, peers // 2, channels, channels), BF16),
            pltpu.VMEM((peers // 4, 3 * channels, 3 * channels), BF16),
            pltpu.VMEM((peers // 4, channels, 4 * channels), BF16),
            pltpu.VMEM((samples, channels), F32),
            pltpu.VMEM((share * peers, rows, channels), F32),
            pltpu.VMEM((peers, rows, channels), F32),
            pltpu.VMEM((samples, channels), F32),
            stack,
            stack,
            stack,
            pltpu.VMEM((faces, block, primal), BF16),
            pltpu.VMEM((faces, block, primal), BF16),
            pltpu.VMEM((samples, primal), BF16),
            pltpu.VMEM((faces, samples, primal), BF16),
            dma((11,)),
            dma((4,)),
            dma((4,)),
            dma((4,)),
            dma((4,)),
            dma((lines,)),
            dma((lines,)),
            dma,
            dma,
            dma,
            dma,
            dma,
            dma,
            dma,
            dma,
            dma((4,)),
            dma((4,)),
            dma((4,)),
            dma((4,)),
            dma((4,)),
            dma((4,)),
        ],
        compiler_params=pltpu.CompilerParams(
            collective_id=0, has_side_effects=True, vmem_limit_bytes=60 * 1024 * 1024
        ),
    )(
        face_slot[0, 0],
        face_scale[0, 0],
        residual_parts[0, 0],
        face_order[0, 0],
        vertex_unknowns[0],
        chain_transfer[0],
        front_inverse[0, 0],
        coarse_basis[0, 0].reshape(faces, block, primal),
        coarse_inverse[0],
        thermal_handoff[0],
        coupling_in[0],
    )
    return out[None, None]


def solution(mesh):
    placed = (
        P("sub", "coarse", None, None, None),
        P("sub", "coarse", None),
        P("sub", "coarse", None, None),
        P("sub", "coarse", None),
        P("sub", "coarse", None),
        P("sub", "coarse", None, None),
        P("sub", "coarse", None, None),
        P("sub", None, "coarse"),
        P("sub", None, None),
        P("sub", None, None),
        P("sub", None, "coarse"),
    )
    return jax.shard_map(
        functools.partial(per_device, mesh.shape["sub"], mesh.shape["coarse"]),
        mesh=mesh,
        in_specs=placed,
        out_specs=P("sub", "coarse", None, None, None),
        check_vma=False,
    )
```
